512 devices in a mesh: row: 32 (over x, z), col: 16 (over y, core).
Axes of the slice: x: 4, y: 8, z: 8, core: 2. Of those that a mesh axis runs over, the one named last changes fastest.
Arguments:
- saved_inputs: bfloat16 [1536, 8192], P('col', 'row'), may hold values from -6 to 6
- out_grad: bfloat16 [1536, 8192], P('col', 'row'), may hold values from -0.59765625 to 0.59765625
- gate_pre: bfloat16 [1536, 14336], P('row', 'col'), may hold values from -8 to 8
- up_pre: bfloat16 [1536, 14336], P('row', 'col'), may hold values from -6 to 6
- gate_weight: bfloat16 [8192, 14336], P('row', 'col'), may hold values from -0.0625 to 0.0625
- up_weight: bfloat16 [8192, 14336], P('row', 'col'), may hold values from -0.0625 to 0.0625
- down_weight: bfloat16 [14336, 8192], P('col', 'row'), may hold values from -0.046875 to 0.046875
Outputs:
- input_grad: bfloat16 [1536, 8192], P('col', 'row')
- gate_grad: bfloat16 [8192, 14336], P('row', 'col')
- up_grad: bfloat16 [8192, 14336], P('row', 'col')
- down_grad: bfloat16 [14336, 8192], P('col', 'row')
The draws below stay inside these ranges and needn't reach their ends.
All inputs are finite; a program needn't handle non-finite values.
Results may differ from the reference program's by a relative error of at most 0.033.
Values may be sent and summed in bfloat16 or wider, within the bound.
No kernel may reach another device: no remote copies, remote signals or barrier semaphores. Data moves between devices by JAX's collectives and lax.ppermute only.
A program may use at most 64 MiB of HBM per device.

```python
import jax
import jax.numpy as jnp
from jax import lax

D = 8192
FF = 14336
TOKENS = 1536
N_ROW = 32
N_COL = 16


def spiked(entries, own_key, source, target, parts, factor):
    def block_of(axis_at):
        return (jnp.arange(entries.shape[axis_at]) // (entries.shape[axis_at] // parts)).reshape((-1,) + (1,) * (entries.ndim - 1 - axis_at))

    one_side = jax.random.permutation(own_key, parts)[block_of(target)]
    other_side = (block_of(target) + parts // 2) % parts
    return jnp.where((block_of(source) == one_side) | (block_of(source) == other_side), factor * entries, entries)


def block_levels(rng, shape, pieces, smallest, largest):
    def one(dim, parts):
        draws = jax.random.uniform(jax.random.fold_in(jax.random.fold_in(rng, 6), dim), (parts,), jnp.float32, smallest / len(pieces), largest / len(pieces))
        return jnp.repeat(jnp.exp(draws), shape[dim] // parts).reshape((-1,) + (1,) * (len(shape) - dim - 1))

    factor_of = one(*pieces[0])
    for cut in pieces[1:]:
        factor_of = factor_of * one(*cut)
    return factor_of


def gaussian(stream_key, extent, scale, bound, cuts=(), kind=jnp.bfloat16):
    values = scale * jax.random.normal(stream_key, extent, jnp.float32)
    if cuts:
        values = values * block_levels(stream_key, extent, cuts, -0.22, 0.18)
    return jnp.clip(values, -bound, bound).astype(kind)


def bell_draw_with(key, extent, spread, most, pieces, heavy, held_as=jnp.bfloat16):
    array = spread * jax.random.normal(key, extent, jnp.float32)
    if pieces:
        array = array * block_levels(key, extent, pieces, -0.22, 0.18)
    return jnp.clip(spiked(array, jax.random.fold_in(key, 3), *heavy), -most, most).astype(held_as)


def setup_inputs(seed: int = 0) -> dict:
    arg_keys = jax.random.split(jax.random.key(seed), 8)
    saved_inputs = gaussian(arg_keys[0], (TOKENS, D), 1.0, 6.0, ((0, 16), (1, 32)))
    out_grad = bell_draw_with(arg_keys[1], (TOKENS, D), 0.1, 0.59765625, ((0, 16), (1, 32)), (1, 0, 32, 2.75))
    gate_pre = gaussian(arg_keys[2], (TOKENS, FF), 1.5, 8.0, ((0, 32), (1, 16)))
    up_pre = gaussian(arg_keys[3], (TOKENS, FF), 1.0, 6.0, ((0, 32), (1, 16)))
    gate_weight = gaussian(arg_keys[4], (D, FF), D ** -0.5, 0.0625, ((0, 32), (1, 16)))
    up_weight = gaussian(arg_keys[5], (D, FF), D ** -0.5, 0.0625, ((0, 32), (1, 16)))
    down_weight = gaussian(arg_keys[6], (FF, D), FF ** -0.5, 0.046875, ((0, 16), (1, 32)))
    return dict(saved_inputs=saved_inputs, out_grad=out_grad, gate_pre=gate_pre, up_pre=up_pre, gate_weight=gate_weight, up_weight=up_weight, down_weight=down_weight)


def reference(saved_inputs, out_grad, gate_pre, up_pre, gate_weight, up_weight, down_weight):
    width_block = D // N_ROW
    hidden_block = FF // N_COL

    def add_hidden(index, total):
        start = (index * width_block).astype(jnp.int32)
        grads = lax.dynamic_slice_in_dim(out_grad, start, width_block, 1)
        weights = lax.dynamic_slice_in_dim(down_weight, start, width_block, 1)
        part = jnp.dot(grads, weights.T, preferred_element_type=jnp.float32)
        return total + part.astype(jnp.bfloat16).astype(jnp.float32)

    hidden_grad = lax.fori_loop(0, N_ROW, add_hidden, jnp.zeros((TOKENS, FF), jnp.float32))
    gate_val = gate_pre.astype(jnp.float32)
    up_val = up_pre.astype(jnp.float32)
    sigma = jax.nn.sigmoid(gate_val)
    silu = gate_val * sigma
    gate_delta = (hidden_grad * up_val * sigma * (1.0 + gate_val * (1.0 - sigma))).astype(jnp.bfloat16)
    up_delta = (hidden_grad * silu).astype(jnp.bfloat16)
    hidden = (silu * up_val).astype(jnp.bfloat16)
    down_grad = jnp.dot(hidden.T, out_grad, preferred_element_type=jnp.float32).astype(jnp.bfloat16)
    gate_grad = jnp.dot(saved_inputs.T, gate_delta, preferred_element_type=jnp.float32).astype(jnp.bfloat16)
    up_grad = jnp.dot(saved_inputs.T, up_delta, preferred_element_type=jnp.float32).astype(jnp.bfloat16)

    def add_input(index, total):
        start = (index * hidden_block).astype(jnp.int32)
        gate_cols = lax.dynamic_slice_in_dim(gate_delta, start, hidden_block, 1)
        up_cols = lax.dynamic_slice_in_dim(up_delta, start, hidden_block, 1)
        gate_w = lax.dynamic_slice_in_dim(gate_weight, start, hidden_block, 1)
        up_w = lax.dynamic_slice_in_dim(up_weight, start, hidden_block, 1)
        term = jnp.dot(gate_cols, gate_w.T, preferred_element_type=jnp.float32)
        term = term + jnp.dot(up_cols, up_w.T, preferred_element_type=jnp.float32)
        return total + term.astype(jnp.bfloat16).astype(jnp.float32)

    input_grad = lax.fori_loop(0, N_COL, add_input, jnp.zeros((TOKENS, D), jnp.float32)).astype(jnp.bfloat16)
    return input_grad, gate_grad, up_grad, down_grad
```

```python
import jax
import jax.numpy as jnp
from jax import lax
from jax.sharding import Mesh, PartitionSpec as P

BF = jnp.bfloat16
F32 = jnp.float32
SWAP = [(0, 1), (1, 0)]


def contract_rows(left, right):
    return lax.dot_general(left, right, (((0,), (0,)), ((), ())), preferred_element_type=F32)


def contract_cols(left, right):
    return lax.dot_general(left, right, (((1,), (1,)), ((), ())), preferred_element_type=F32)


def swap(value):
    return lax.ppermute(value, "zw", SWAP)


def halves(value, w):
    n = value.shape[0] // 2
    return (
        lax.dynamic_slice_in_dim(value, w * n, n, 0),
        lax.dynamic_slice_in_dim(value, (1 - w) * n, n, 0),
    )


def gather_tokens(value, w):
    mine, theirs = halves(value, w)
    both = jnp.concatenate([mine, swap(theirs)], axis=1)
    return lax.all_gather(both, ("y", "core"), axis=0, tiled=True)


def scatter_sum(value, axis, parts):
    arrived = lax.all_to_all(value, axis, 0, 0, tiled=True)
    return arrived.astype(F32).sum(axis=0)


def weight_grad(partial, n, axis):
    own = lax.slice_in_dim(partial, 0, n, axis=axis)
    other = lax.slice_in_dim(partial, n, 2 * n, axis=axis)
    return (own + swap(other.astype(BF)).astype(F32)).astype(BF)


def body(saved_inputs, out_grad, gate_pre, up_pre, gate_weight, up_weight, down_weight):
    w = lax.axis_index("zw")
    width = out_grad.shape[1]
    tokens = gate_pre.shape[0]
    units = gate_pre.shape[1]
    down_w = jnp.concatenate([down_weight, swap(down_weight)], axis=1)
    grads = gather_tokens(out_grad, w)
    pre = lax.all_gather(
        jnp.concatenate([gate_pre, up_pre], axis=1), ("x", "zq"), axis=0, tiled=True
    )
    gate_w = jnp.concatenate([gate_weight, swap(gate_weight)], axis=0)
    up_w = jnp.concatenate([up_weight, swap(up_weight)], axis=0)

    part = contract_cols(grads, down_w).astype(BF)
    part = scatter_sum(part.reshape(4, 4 * tokens, units), "x", 4).astype(BF)
    part = scatter_sum(part.reshape(4, tokens, units), "zq", 4).astype(BF)
    hidden_grad = lax.all_to_all(
        jnp.broadcast_to(part[None], (4,) + part.shape), "zq", 0, 0, tiled=True
    ).reshape(4 * tokens, units)
    hidden_grad = lax.all_to_all(
        jnp.broadcast_to(hidden_grad[None], (4,) + hidden_grad.shape), "x", 0, 0, tiled=True
    ).reshape(16 * tokens, units)

    inputs = gather_tokens(saved_inputs, w)
    gate_val = pre[:, :units].astype(F32)
    up_val = pre[:, units:].astype(F32)
    sigma = jax.nn.sigmoid(gate_val)
    silu = gate_val * sigma
    hidden = (silu * up_val).astype(BF)
    hidden_grad = hidden_grad.astype(F32)
    gate_delta = (hidden_grad * up_val * sigma * (1.0 + gate_val * (1.0 - sigma))).astype(BF)
    up_delta = (hidden_grad * silu).astype(BF)

    down_grad = weight_grad(contract_rows(hidden, grads), width, 1)
    term = (contract_cols(gate_delta, gate_w) + contract_cols(up_delta, up_w)).astype(BF)
    term = lax.all_to_all(term.reshape(8, 2, tokens, 2 * width), "core", 1, 1, tiled=True)
    term = term.astype(F32).sum(axis=1).astype(BF)
    term = scatter_sum(term, "y", 8).astype(BF)
    gate_grad = weight_grad(contract_rows(inputs, gate_delta), width, 0)
    up_grad = weight_grad(contract_rows(inputs, up_delta), width, 0)

    mine, theirs = term[:, :width], swap(term[:, width:])
    input_grad = jnp.where(
        w == 0,
        jnp.concatenate([mine, theirs], axis=0),
        jnp.concatenate([theirs, mine], axis=0),
    )
    return (input_grad, gate_grad, up_grad, down_grad)


def solution(mesh):
    fine = Mesh(mesh.devices.reshape(4, 4, 2, 8, 2), ("x", "zq", "zw", "y", "core"))
    row, col = ("x", "zq", "zw"), ("y", "core")
    return jax.shard_map(
        body,
        mesh=fine,
        in_specs=(
            P(col, row),
            P(col, row),
            P(row, col),
            P(row, col),
            P(row, col),
            P(row, col),
            P(col, row),
        ),
        out_specs=(P(col, row), P(row, col), P(row, col), P(col, row)),
        check_vma=False,
    )
```

```python
import jax
import jax.numpy as jnp
from jax import lax
from jax.sharding import Mesh, PartitionSpec as P

BF = jnp.bfloat16
F32 = jnp.float32
SWAP = [(0, 1), (1, 0)]


def contract_rows(left, right):
    return lax.dot_general(left, right, (((0,), (0,)), ((), ())), preferred_element_type=F32)


def contract_cols(left, right):
    return lax.dot_general(left, right, (((1,), (1,)), ((), ())), preferred_element_type=F32)


def swap(value):
    return lax.ppermute(value, "zw", SWAP)


def halves(value, w):
    n = value.shape[0] // 2
    return (
        lax.dynamic_slice_in_dim(value, w * n, n, 0),
        lax.dynamic_slice_in_dim(value, (1 - w) * n, n, 0),
    )


def pair_columns(value, w):
    mine, theirs = halves(value, w)
    return in_order(mine, swap(theirs), w, 1)


def spread(value, axis, parts):
    copies = jnp.broadcast_to(value[None], (parts,) + value.shape)
    return lax.all_to_all(copies, axis, 0, 0, tiled=True).reshape((-1,) + value.shape[1:])


def scatter_sum(value, axis):
    return lax.all_to_all(value, axis, 0, 0, tiled=True).astype(F32).sum(axis=0)


def in_order(own, other, index, axis):
    return jnp.where(
        index == 0,
        jnp.concatenate([own, other], axis=axis),
        jnp.concatenate([other, own], axis=axis),
    )


def tie(*values):
    return lax.optimization_barrier(values)


def body(saved_inputs, out_grad, gate_pre, up_pre, gate_weight, up_weight, down_weight):
    w = lax.axis_index("zw")
    c = lax.axis_index("core")
    width = out_grad.shape[1]
    tokens, units = gate_pre.shape

    rows = jnp.concatenate([out_grad, saved_inputs], axis=1).reshape(2, 1, tokens, 2 * width)
    rows = jnp.broadcast_to(rows, (2, 8, tokens, 2 * width)).reshape(16, tokens, 2 * width)
    rows, down_weight = tie(rows, down_weight)
    rows = lax.all_to_all(rows, ("zw", "y"), 0, 0, tiled=True)
    rows = rows.reshape(2, 8, 1, tokens, 2 * width)
    down_w = swap(down_weight)
    rows, down_w = tie(rows, down_w)
    down_w = jnp.concatenate([down_weight, down_w], axis=1)
    rows = in_order(rows, lax.ppermute(rows, "core", SWAP), c, 2)
    own, other = (
        lax.dynamic_index_in_dim(rows, i, 0, keepdims=False).reshape(16 * tokens, 2 * width)
        for i in (w, 1 - w)
    )
    grads = jnp.concatenate([own[:, :width], other[:, :width]], axis=1)

    part = contract_cols(grads, down_w).astype(BF)
    part, gate_pre, up_pre, own, other = tie(part, gate_pre, up_pre, own, other)
    pre = jnp.concatenate([gate_pre, up_pre], axis=1)
    pre = lax.all_gather(pre, "zq", axis=0, tiled=True)
    part = scatter_sum(part.reshape(4, 4 * tokens, units), "x").astype(BF)
    part, pre, gate_weight, up_weight = tie(part, pre, gate_weight, up_weight)
    pre = lax.all_gather(pre, "x", axis=0, tiled=True)
    own, other = own[:, width:], other[:, width:]
    part = scatter_sum(part.reshape(4, tokens, units), "zq").astype(BF)
    both_w = jnp.concatenate([gate_weight, up_weight], axis=1)
    part, own, other = tie(part, own, other)
    hidden_grad = spread(part, "zq", 4)
    hidden_grad, both_w = tie(hidden_grad, both_w)
    hidden_grad = spread(hidden_grad, "x", 4)
    both_w_other = swap(both_w)

    gate_val = pre[:, :units].astype(F32)
    up_val = pre[:, units:].astype(F32)
    sigma = jax.nn.sigmoid(gate_val)
    silu = gate_val * sigma
    hidden = (silu * up_val).astype(BF)
    down_other = contract_rows(hidden, grads[:, width:]).astype(BF)
    hidden_grad, down_other, pre = tie(hidden_grad, down_other, pre)
    down_other = swap(down_other)

    gate_val = pre[:, :units].astype(F32)
    up_val = pre[:, units:].astype(F32)
    sigma = jax.nn.sigmoid(gate_val)
    silu = gate_val * sigma
    hidden_grad = hidden_grad.astype(F32)
    gate_delta = hidden_grad * up_val * sigma * (1.0 + gate_val * (1.0 - sigma))
    up_delta = hidden_grad * silu
    both = jnp.concatenate([gate_delta.astype(BF), up_delta.astype(BF)], axis=1)
    sums_other = contract_rows(other, both).astype(BF)
    both, sums_other = tie(both, sums_other)
    sums_other = swap(sums_other)
    term = [contract_cols(both, m).astype(BF) for m in (both_w, both_w_other)]
    term = [t.reshape(8, 2, tokens, width).transpose(1, 0, 2, 3) for t in term]
    term = jnp.where(w == 0, jnp.stack(term, axis=1), jnp.stack(term[::-1], axis=1))
    term = lax.all_to_all(term, "core", 0, 0, tiled=True)
    term = term.astype(F32).sum(axis=0).astype(BF).reshape(16, tokens, width)
    term = lax.all_to_all(term, ("zw", "y"), 0, 0, tiled=True)
    gate_grad = (contract_rows(own, both[:, :units]) + sums_other[:, :units].astype(F32)).astype(BF)
    up_grad = (contract_rows(own, both[:, units:]) + sums_other[:, units:].astype(F32)).astype(BF)
    down_grad = (contract_rows(hidden, grads[:, :width]) + down_other.astype(F32)).astype(BF)
    term, gate_grad, up_grad = tie(term, gate_grad, up_grad)
    input_grad = term.astype(F32).reshape(2, 8, tokens, width).sum(axis=1).astype(BF)
    return (input_grad.reshape(2 * tokens, width), gate_grad, up_grad, down_grad)


def solution(mesh):
    fine = Mesh(mesh.devices.reshape(4, 4, 2, 8, 2), ("x", "zq", "zw", "y", "core"))
    row, col = ("x", "zq", "zw"), ("y", "core")
    return jax.shard_map(
        body,
        mesh=fine,
        in_specs=(
            P(col, row),
            P(col, row),
            P(row, col),
            P(row, col),
            P(row, col),
            P(row, col),
            P(col, row),
        ),
        out_specs=(P(col, row), P(row, col), P(row, col), P(col, row)),
        check_vma=False,
    )
```

```python
import jax
import jax.numpy as jnp
from jax import lax
from jax.sharding import Mesh, PartitionSpec as P

BF = jnp.bfloat16
F32 = jnp.float32
SWAP = [(0, 1), (1, 0)]


def contract_rows(left, right):
    return lax.dot_general(left, right, (((0,), (0,)), ((), ())), preferred_element_type=F32)


def contract_cols(left, right):
    return lax.dot_general(left, right, (((1,), (1,)), ((), ())), preferred_element_type=F32)


def swap(value):
    return lax.ppermute(value, "zw", SWAP)


def halves(value, w):
    n = value.shape[0] // 2
    return (
        lax.dynamic_slice_in_dim(value, w * n, n, 0),
        lax.dynamic_slice_in_dim(value, (1 - w) * n, n, 0),
    )


def pair_columns(value, w):
    mine, theirs = halves(value, w)
    return in_order(mine, swap(theirs), w, 1)


def spread(value, axis, parts):
    copies = jnp.broadcast_to(value[None], (parts,) + value.shape)
    return lax.all_to_all(copies, axis, 0, 0, tiled=True).reshape((-1,) + value.shape[1:])


def pieces(value, axis, parts):
    up = [(i, (i + 1) % parts) for i in range(parts)]
    down = [(i, (i + parts - 1) % parts) for i in range(parts)]
    before = lax.ppermute(value, axis, up)
    after = lax.ppermute(value, axis, down)
    return [before, lax.ppermute(after, axis, down), after]


def assemble(value, others, axis):
    me, parts = lax.axis_index(axis), len(others) + 1
    out = jnp.zeros((parts,) + value.shape, value.dtype)
    for k, piece in enumerate([value] + others):
        out = lax.dynamic_update_index_in_dim(out, piece, (me + parts - k) % parts, 0)
    return out.reshape((-1,) + value.shape[1:])


def scatter_sum(value, axis):
    return lax.all_to_all(value, axis, 0, 0, tiled=True).astype(F32).sum(axis=0)


def in_order(own, other, index, axis):
    return jnp.where(
        index == 0,
        jnp.concatenate([own, other], axis=axis),
        jnp.concatenate([other, own], axis=axis),
    )


def tie(*values):
    return lax.optimization_barrier(values)


def body(saved_inputs, out_grad, gate_pre, up_pre, gate_weight, up_weight, down_weight):
    w = lax.axis_index("zw")
    c = lax.axis_index("core")
    width = out_grad.shape[1]
    tokens, units = gate_pre.shape

    rows = jnp.concatenate([out_grad, saved_inputs], axis=1).reshape(2, 1, tokens, 2 * width)
    rows = jnp.broadcast_to(rows, (2, 8, tokens, 2 * width)).reshape(16, tokens, 2 * width)
    rows, down_weight = tie(rows, down_weight)
    rows = lax.all_to_all(rows, ("zw", "y"), 0, 0, tiled=True)
    rows = rows.reshape(2, 8, 1, tokens, 2 * width)
    down_w = swap(down_weight)
    rows, down_w = tie(rows, down_w)
    down_w = jnp.concatenate([down_weight, down_w], axis=1)
    rows = in_order(rows, lax.ppermute(rows, "core", SWAP), c, 2)
    own, other = (
        lax.dynamic_index_in_dim(rows, i, 0, keepdims=False).reshape(16 * tokens, 2 * width)
        for i in (w, 1 - w)
    )
    grads = jnp.concatenate([own[:, :width], other[:, :width]], axis=1)

    part = contract_cols(grads, down_w).astype(BF)
    part, gate_pre, up_pre, own, other = tie(part, gate_pre, up_pre, own, other)
    pre = jnp.concatenate([gate_pre, up_pre], axis=1)
    pre = lax.all_gather(pre, "zq", axis=0, tiled=True)
    part = scatter_sum(part.reshape(4, 4 * tokens, units), "x").astype(BF)
    part, pre, gate_weight, up_weight = tie(part, pre, gate_weight, up_weight)
    pre_pieces = pieces(pre, "x", 4)
    own, other = own[:, width:], other[:, width:]
    part = scatter_sum(part.reshape(4, tokens, units), "zq").astype(BF)
    both_w = jnp.concatenate([gate_weight, up_weight], axis=1)
    part, own, other = tie(part, own, other)
    hidden_grad = spread(part, "zq", 4)
    hidden_grad, both_w, pre = tie(hidden_grad, both_w, pre)
    hidden_grad = spread(hidden_grad, "x", 4)
    both_w_other = swap(both_w)

    pre = assemble(pre, pre_pieces, "x")
    gate_val = pre[:, :units].astype(F32)
    up_val = pre[:, units:].astype(F32)
    sigma = jax.nn.sigmoid(gate_val)
    silu = gate_val * sigma
    hidden = (silu * up_val).astype(BF)
    down_other = contract_rows(hidden, grads[:, width:]).astype(BF)
    hidden_grad, down_other, pre = tie(hidden_grad, down_other, pre)
    down_other = swap(down_other)

    gate_val = pre[:, :units].astype(F32)
    up_val = pre[:, units:].astype(F32)
    sigma = jax.nn.sigmoid(gate_val)
    silu = gate_val * sigma
    hidden_grad = hidden_grad.astype(F32)
    gate_delta = hidden_grad * up_val * sigma * (1.0 + gate_val * (1.0 - sigma))
    up_delta = hidden_grad * silu
    both = jnp.concatenate([gate_delta.astype(BF), up_delta.astype(BF)], axis=1)
    sums_other = contract_rows(other, both).astype(BF)
    both, sums_other = tie(both, sums_other)
    sums_other = swap(sums_other)
    term = [contract_cols(both, m).astype(BF) for m in (both_w, both_w_other)]
    term = [t.reshape(8, 2, tokens, width).transpose(1, 0, 2, 3) for t in term]
    term = jnp.where(w == 0, jnp.stack(term, axis=1), jnp.stack(term[::-1], axis=1))
    term = lax.all_to_all(term, "core", 0, 0, tiled=True)
    term = term.astype(F32).sum(axis=0).astype(BF).reshape(16, tokens, width)
    term = lax.all_to_all(term, ("zw", "y"), 0, 0, tiled=True)
    gate_grad = (contract_rows(own, both[:, :units]) + sums_other[:, :units].astype(F32)).astype(BF)
    up_grad = (contract_rows(own, both[:, units:]) + sums_other[:, units:].astype(F32)).astype(BF)
    down_grad = (contract_rows(hidden, grads[:, :width]) + down_other.astype(F32)).astype(BF)
    term, gate_grad, up_grad = tie(term, gate_grad, up_grad)
    input_grad = term.astype(F32).reshape(2, 8, tokens, width).sum(axis=1).astype(BF)
    return (input_grad.reshape(2 * tokens, width), gate_grad, up_grad, down_grad)


def solution(mesh):
    fine = Mesh(mesh.devices.reshape(4, 4, 2, 8, 2), ("x", "zq", "zw", "y", "core"))
    row, col = ("x", "zq", "zw"), ("y", "core")
    return jax.shard_map(
        body,
        mesh=fine,
        in_specs=(
            P(col, row),
            P(col, row),
            P(row, col),
            P(row, col),
            P(row, col),
            P(row, col),
            P(col, row),
        ),
        out_specs=(P(col, row), P(row, col), P(row, col), P(col, row)),
        check_vma=False,
    )
```

```python
import jax
import jax.numpy as jnp
from jax import lax
from jax.sharding import Mesh, PartitionSpec as P

BF = jnp.bfloat16
F32 = jnp.float32
SWAP = [(0, 1), (1, 0)]


def contract_rows(left, right):
    return lax.dot_general(left, right, (((0,), (0,)), ((), ())), preferred_element_type=F32)


def contract_cols(left, right):
    return lax.dot_general(left, right, (((1,), (1,)), ((), ())), preferred_element_type=F32)


def swap(value):
    return lax.ppermute(value, "zw", SWAP)


def halves(value, w):
    n = value.shape[0] // 2
    return (
        lax.dynamic_slice_in_dim(value, w * n, n, 0),
        lax.dynamic_slice_in_dim(value, (1 - w) * n, n, 0),
    )


def pair_columns(value, w):
    mine, theirs = halves(value, w)
    return in_order(mine, swap(theirs), w, 1)


def spread(value, axis, parts):
    copies = jnp.broadcast_to(value[None], (parts,) + value.shape)
    return lax.all_to_all(copies, axis, 0, 0, tiled=True).reshape((-1,) + value.shape[1:])


def pieces(value, axis, parts):
    up = [(i, (i + 1) % parts) for i in range(parts)]
    down = [(i, (i + parts - 1) % parts) for i in range(parts)]
    before = lax.ppermute(value, axis, up)
    after = lax.ppermute(value, axis, down)
    return [before, lax.ppermute(after, axis, down), after]


def assemble(value, others, axis):
    me, parts = lax.axis_index(axis), len(others) + 1
    out = jnp.zeros((parts,) + value.shape, value.dtype)
    for k, piece in enumerate([value] + others):
        out = lax.dynamic_update_index_in_dim(out, piece, (me + parts - k) % parts, 0)
    return out.reshape((-1,) + value.shape[1:])


def scatter_sum(value, axis):
    return lax.all_to_all(value, axis, 0, 0, tiled=True).astype(F32).sum(axis=0)


def in_order(own, other, index, axis):
    return jnp.where(
        index == 0,
        jnp.concatenate([own, other], axis=axis),
        jnp.concatenate([other, own], axis=axis),
    )


def tie(*values):
    return lax.optimization_barrier(values)


def body(saved_inputs, out_grad, gate_pre, up_pre, gate_weight, up_weight, down_weight):
    w = lax.axis_index("zw")
    c = lax.axis_index("core")
    width = out_grad.shape[1]
    tokens, units = gate_pre.shape

    rows = jnp.concatenate([out_grad, saved_inputs], axis=1).reshape(2, 1, tokens, 2 * width)
    rows = jnp.broadcast_to(rows, (2, 8, tokens, 2 * width)).reshape(16, tokens, 2 * width)
    rows, down_weight = tie(rows, down_weight)
    rows = lax.all_to_all(rows, ("zw", "y"), 0, 0, tiled=True)
    rows = rows.reshape(2, 8, 1, tokens, 2 * width)
    down_w = swap(down_weight)
    rows, down_w = tie(rows, down_w)
    down_w = jnp.concatenate([down_weight, down_w], axis=1)
    rows = in_order(rows, lax.ppermute(rows, "core", SWAP), c, 2)
    own, other = (
        lax.dynamic_index_in_dim(rows, i, 0, keepdims=False).reshape(16 * tokens, 2 * width)
        for i in (w, 1 - w)
    )
    grads = jnp.concatenate([own[:, :width], other[:, :width]], axis=1)

    part = contract_cols(grads, down_w).astype(BF)
    part, gate_pre, up_pre, own, other = tie(part, gate_pre, up_pre, own, other)
    pre = jnp.concatenate([gate_pre, up_pre], axis=1)
    pre = lax.all_gather(pre, "zq", axis=0, tiled=True)
    part = scatter_sum(part.reshape(4, 4 * tokens, units), "x").astype(BF)
    part, pre, gate_weight, up_weight = tie(part, pre, gate_weight, up_weight)
    pre_pieces = pieces(pre, "x", 4)
    own, other = own[:, width:], other[:, width:]
    part = scatter_sum(part.reshape(4, tokens, units), "zq").astype(BF)
    both_w = jnp.concatenate([gate_weight, up_weight], axis=1)
    part, own, other = tie(part, own, other)
    hidden_grad = spread(part, "zq", 4)
    hidden_grad, both_w, pre, gate_weight, up_weight = tie(
        hidden_grad, both_w, pre, gate_weight, up_weight
    )
    hidden_grad = spread(hidden_grad, "x", 4)
    both_w_other = swap(both_w)
    both_w = jnp.concatenate([gate_weight, up_weight], axis=1)

    pre = assemble(pre, pre_pieces, "x")
    gate_val = pre[:, :units].astype(F32)
    up_val = pre[:, units:].astype(F32)
    sigma = jax.nn.sigmoid(gate_val)
    silu = gate_val * sigma
    hidden = (silu * up_val).astype(BF)
    down_other = contract_rows(hidden, grads[:, width:]).astype(BF)
    hidden_grad, down_other, pre, both_w = tie(hidden_grad, down_other, pre, both_w)
    down_other = swap(down_other)

    gate_val = pre[:, :units].astype(F32)
    up_val = pre[:, units:].astype(F32)
    sigma = jax.nn.sigmoid(gate_val)
    silu = gate_val * sigma
    hidden_grad = hidden_grad.astype(F32)
    gate_delta = hidden_grad * up_val * sigma * (1.0 + gate_val * (1.0 - sigma))
    up_delta = hidden_grad * silu
    both = jnp.concatenate([gate_delta.astype(BF), up_delta.astype(BF)], axis=1)
    sums_other = contract_rows(other, both).astype(BF)
    both, sums_other = tie(both, sums_other)
    sums_other = swap(sums_other)
    term = [contract_cols(both, m).astype(BF) for m in (both_w, both_w_other)]
    term = [t.reshape(8, 2, tokens, width).transpose(1, 0, 2, 3) for t in term]
    term = jnp.where(w == 0, jnp.stack(term, axis=1), jnp.stack(term[::-1], axis=1))
    term = lax.all_to_all(term, "core", 0, 0, tiled=True)
    term = term.astype(F32).sum(axis=0).astype(BF).reshape(16, tokens, width)
    term = lax.all_to_all(term, ("zw", "y"), 0, 0, tiled=True)
    gate_grad = (contract_rows(own, both[:, :units]) + sums_other[:, :units].astype(F32)).astype(BF)
    up_grad = (contract_rows(own, both[:, units:]) + sums_other[:, units:].astype(F32)).astype(BF)
    down_grad = (contract_rows(hidden, grads[:, :width]) + down_other.astype(F32)).astype(BF)
    term, gate_grad, up_grad = tie(term, gate_grad, up_grad)
    input_grad = term.astype(F32).reshape(2, 8, tokens, width).sum(axis=1).astype(BF)
    return (input_grad.reshape(2 * tokens, width), gate_grad, up_grad, down_grad)


def solution(mesh):
    fine = Mesh(mesh.devices.reshape(4, 4, 2, 8, 2), ("x", "zq", "zw", "y", "core"))
    row, col = ("x", "zq", "zw"), ("y", "core")
    return jax.shard_map(
        body,
        mesh=fine,
        in_specs=(
            P(col, row),
            P(col, row),
            P(row, col),
            P(row, col),
            P(row, col),
            P(row, col),
            P(col, row),
        ),
        out_specs=(P(col, row), P(row, col), P(row, col), P(col, row)),
        check_vma=False,
    )
```

```python
import jax
import jax.numpy as jnp
from jax import lax
from jax.sharding import Mesh, PartitionSpec as P

BF = jnp.bfloat16
F32 = jnp.float32
SWAP = [(0, 1), (1, 0)]


def contract_rows(left, right):
    return lax.dot_general(left, right, (((0,), (0,)), ((), ())), preferred_element_type=F32)


def contract_cols(left, right):
    return lax.dot_general(left, right, (((1,), (1,)), ((), ())), preferred_element_type=F32)


def swap(value):
    return lax.ppermute(value, "zw", SWAP)


def halves(value, w):
    n = value.shape[0] // 2
    return (
        lax.dynamic_slice_in_dim(value, w * n, n, 0),
        lax.dynamic_slice_in_dim(value, (1 - w) * n, n, 0),
    )


def pair_columns(value, w):
    mine, theirs = halves(value, w)
    return in_order(mine, swap(theirs), w, 1)


def spread(value, axis, parts):
    copies = jnp.broadcast_to(value[None], (parts,) + value.shape)
    return lax.all_to_all(copies, axis, 0, 0, tiled=True).reshape((-1,) + value.shape[1:])


def pieces(value, axis, parts):
    up = [(i, (i + 1) % parts) for i in range(parts)]
    down = [(i, (i + parts - 1) % parts) for i in range(parts)]
    before = lax.ppermute(value, axis, up)
    after = lax.ppermute(value, axis, down)
    return [before, lax.ppermute(after, axis, down), after]


def assemble(value, others, axis):
    me, parts = lax.axis_index(axis), len(others) + 1
    out = jnp.zeros((parts,) + value.shape, value.dtype)
    for k, piece in enumerate([value] + others):
        out = lax.dynamic_update_index_in_dim(out, piece, (me + parts - k) % parts, 0)
    return out.reshape((-1,) + value.shape[1:])


def scatter_sum(value, axis):
    return lax.all_to_all(value, axis, 0, 0, tiled=True).astype(F32).sum(axis=0)


def in_order(own, other, index, axis):
    return jnp.where(
        index == 0,
        jnp.concatenate([own, other], axis=axis),
        jnp.concatenate([other, own], axis=axis),
    )


def tie(*values):
    return lax.optimization_barrier(values)


def body(saved_inputs, out_grad, gate_pre, up_pre, gate_weight, up_weight, down_weight):
    w = lax.axis_index("zw")
    c = lax.axis_index("core")
    width = out_grad.shape[1]
    tokens, units = gate_pre.shape

    rows = jnp.concatenate([out_grad, saved_inputs], axis=1).reshape(2, 1, tokens, 2 * width)
    rows = jnp.broadcast_to(rows, (2, 8, tokens, 2 * width)).reshape(16, tokens, 2 * width)
    rows, down_weight = tie(rows, down_weight)
    rows = lax.all_to_all(rows, ("zw", "y"), 0, 0, tiled=True)
    rows = rows.reshape(2, 8, 1, tokens, 2 * width)
    down_w = swap(down_weight)
    rows, down_w = tie(rows, down_w)
    down_w = jnp.concatenate([down_weight, down_w], axis=1)
    rows = in_order(rows, lax.ppermute(rows, "core", SWAP), c, 2)
    own, other = (
        lax.dynamic_index_in_dim(rows, i, 0, keepdims=False).reshape(16 * tokens, 2 * width)
        for i in (w, 1 - w)
    )
    grads = jnp.concatenate([own[:, :width], other[:, :width]], axis=1)

    part = contract_cols(grads, down_w).astype(BF)
    part, gate_pre, up_pre, own, other = tie(part, gate_pre, up_pre, own, other)
    pre = jnp.concatenate([gate_pre, up_pre], axis=1)
    pre = lax.all_gather(pre, "zq", axis=0, tiled=True)
    part = scatter_sum(part.reshape(4, 4 * tokens, units), "x").astype(BF)
    part, pre, gate_weight, up_weight = tie(part, pre, gate_weight, up_weight)
    pre_pieces = pieces(pre, "x", 4)
    own, other = own[:, width:], other[:, width:]
    part = scatter_sum(part.reshape(4, tokens, units), "zq").astype(BF)
    both_w = jnp.concatenate([gate_weight, up_weight], axis=1)
    part, own, other = tie(part, own, other)
    hidden_grad = spread(part, "zq", 4)
    hidden_grad, both_w, pre, gate_weight, up_weight = tie(
        hidden_grad, both_w, pre, gate_weight, up_weight
    )
    hidden_grad = spread(hidden_grad, "x", 4)
    both_w_other = swap(both_w)
    both_w = jnp.concatenate([gate_weight, up_weight], axis=1)

    pre = assemble(pre, pre_pieces, "x")
    gate_val = pre[:, :units].astype(F32)
    up_val = pre[:, units:].astype(F32)
    sigma = jax.nn.sigmoid(gate_val)
    silu = gate_val * sigma
    hidden = (silu * up_val).astype(BF)
    gate_scale = (up_val * sigma * (1.0 + gate_val * (1.0 - sigma))).astype(BF)
    up_scale = silu.astype(BF)
    down_other = contract_rows(hidden, grads[:, width:]).astype(BF)
    hidden_grad, down_other, gate_scale, up_scale, both_w = tie(
        hidden_grad, down_other, gate_scale, up_scale, both_w
    )
    down_other = swap(down_other)
    hidden_grad = hidden_grad.astype(F32)
    gate_delta = (hidden_grad * gate_scale.astype(F32)).astype(BF)
    up_delta = (hidden_grad * up_scale.astype(F32)).astype(BF)
    both = jnp.concatenate([gate_delta, up_delta], axis=1)
    sums_other = contract_rows(other, both).astype(BF)
    both, sums_other = tie(both, sums_other)
    sums_other = swap(sums_other)
    term = [contract_cols(both, m).astype(BF) for m in (both_w, both_w_other)]
    term = [t.reshape(8, 2, tokens, width).transpose(1, 0, 2, 3) for t in term]
    term = jnp.where(w == 0, jnp.stack(term, axis=1), jnp.stack(term[::-1], axis=1))
    term = lax.all_to_all(term, "core", 0, 0, tiled=True)
    term = term.astype(F32).sum(axis=0).astype(BF).reshape(16, tokens, width)
    term = lax.all_to_all(term, ("zw", "y"), 0, 0, tiled=True)
    gate_grad = (contract_rows(own, both[:, :units]) + sums_other[:, :units].astype(F32)).astype(BF)
    up_grad = (contract_rows(own, both[:, units:]) + sums_other[:, units:].astype(F32)).astype(BF)
    down_grad = (contract_rows(hidden, grads[:, :width]) + down_other.astype(F32)).astype(BF)
    term, gate_grad, up_grad = tie(term, gate_grad, up_grad)
    input_grad = term.astype(F32).reshape(2, 8, tokens, width).sum(axis=1).astype(BF)
    return (input_grad.reshape(2 * tokens, width), gate_grad, up_grad, down_grad)


def solution(mesh):
    fine = Mesh(mesh.devices.reshape(4, 4, 2, 8, 2), ("x", "zq", "zw", "y", "core"))
    row, col = ("x", "zq", "zw"), ("y", "core")
    return jax.shard_map(
        body,
        mesh=fine,
        in_specs=(
            P(col, row),
            P(col, row),
            P(row, col),
            P(row, col),
            P(row, col),
            P(row, col),
            P(col, row),
        ),
        out_specs=(P(col, row), P(row, col), P(row, col), P(col, row)),
        check_vma=False,
    )
```

```python
import jax
import jax.numpy as jnp
from jax import lax
from jax.sharding import Mesh, PartitionSpec as P

BF = jnp.bfloat16
F32 = jnp.float32
SWAP = [(0, 1), (1, 0)]


def contract_rows(left, right):
    return lax.dot_general(left, right, (((0,), (0,)), ((), ())), preferred_element_type=F32)


def contract_cols(left, right):
    return lax.dot_general(left, right, (((1,), (1,)), ((), ())), preferred_element_type=F32)


def swap(value):
    return lax.ppermute(value, "zw", SWAP)


def halves(value, w):
    n = value.shape[0] // 2
    return (
        lax.dynamic_slice_in_dim(value, w * n, n, 0),
        lax.dynamic_slice_in_dim(value, (1 - w) * n, n, 0),
    )


def pair_columns(value, w):
    mine, theirs = halves(value, w)
    return in_order(mine, swap(theirs), w, 1)


def spread(value, axis, parts):
    copies = jnp.broadcast_to(value[None], (parts,) + value.shape)
    return lax.all_to_all(copies, axis, 0, 0, tiled=True).reshape((-1,) + value.shape[1:])


def pieces(value, axis, parts):
    up = [(i, (i + 1) % parts) for i in range(parts)]
    down = [(i, (i + parts - 1) % parts) for i in range(parts)]
    before = lax.ppermute(value, axis, up)
    after = lax.ppermute(value, axis, down)
    return [before, lax.ppermute(after, axis, down), after]


def assemble(value, others, axis):
    me, parts = lax.axis_index(axis), len(others) + 1
    out = jnp.zeros((parts,) + value.shape, value.dtype)
    for k, piece in enumerate([value] + others):
        out = lax.dynamic_update_index_in_dim(out, piece, (me + parts - k) % parts, 0)
    return out.reshape((-1,) + value.shape[1:])


def scatter_sum(value, axis):
    return lax.all_to_all(value, axis, 0, 0, tiled=True).astype(F32).sum(axis=0)


def in_order(own, other, index, axis):
    return jnp.where(
        index == 0,
        jnp.concatenate([own, other], axis=axis),
        jnp.concatenate([other, own], axis=axis),
    )


def tie(*values):
    return lax.optimization_barrier(values)


def body(saved_inputs, out_grad, gate_pre, up_pre, gate_weight, up_weight, down_weight):
    w = lax.axis_index("zw")
    c = lax.axis_index("core")
    width = out_grad.shape[1]
    tokens, units = gate_pre.shape

    rows = jnp.concatenate([out_grad, saved_inputs], axis=1).reshape(2, 1, tokens, 2 * width)
    rows = jnp.broadcast_to(rows, (2, 8, tokens, 2 * width)).reshape(16, tokens, 2 * width)
    rows, down_weight = tie(rows, down_weight)
    rows = lax.all_to_all(rows, ("zw", "y"), 0, 0, tiled=True)
    rows = rows.reshape(2, 8, 1, tokens, 2 * width)
    down_w = swap(down_weight)
    rows, down_w = tie(rows, down_w)
    down_w = jnp.concatenate([down_weight, down_w], axis=1)
    rows = in_order(rows, lax.ppermute(rows, "core", SWAP), c, 2)
    own, other = (
        lax.dynamic_index_in_dim(rows, i, 0, keepdims=False).reshape(16 * tokens, 2 * width)
        for i in (w, 1 - w)
    )
    grads = jnp.concatenate([own[:, :width], other[:, :width]], axis=1)

    part = contract_cols(grads, down_w).astype(BF)
    part, gate_pre, up_pre, own, other = tie(part, gate_pre, up_pre, own, other)
    pre = jnp.concatenate([gate_pre, up_pre], axis=1)
    pre = lax.all_gather(pre, "zq", axis=0, tiled=True)
    part = scatter_sum(part.reshape(4, 4 * tokens, units), "x").astype(BF)
    part, pre, gate_weight, up_weight = tie(part, pre, gate_weight, up_weight)
    pre_pieces = pieces(pre, "x", 4)
    own, other = own[:, width:], other[:, width:]
    part = scatter_sum(part.reshape(4, tokens, units), "zq").astype(BF)
    both_w = jnp.concatenate([gate_weight, up_weight], axis=1)
    part, own, other, both_w = tie(part, own, other, both_w)
    hidden_grad = spread(part, "zq", 4)
    hidden_grad, both_w, pre, gate_weight, up_weight = tie(
        hidden_grad, both_w, pre, gate_weight, up_weight
    )
    hidden_grad = spread(hidden_grad, "x", 4)
    both_w_other = swap(both_w)
    both_w = jnp.concatenate([gate_weight, up_weight], axis=1)

    pre = assemble(pre, pre_pieces, "x")
    gate_val = pre[:, :units].astype(F32)
    up_val = pre[:, units:].astype(F32)
    sigma = jax.nn.sigmoid(gate_val)
    silu = gate_val * sigma
    hidden = (silu * up_val).astype(BF)
    down_other = contract_rows(hidden, grads[:, width:]).astype(BF)
    hidden_grad, down_other, pre, both_w = tie(hidden_grad, down_other, pre, both_w)
    down_other = swap(down_other)

    gate_val = pre[:, :units].astype(F32)
    up_val = pre[:, units:].astype(F32)
    sigma = jax.nn.sigmoid(gate_val)
    silu = gate_val * sigma
    hidden_grad = hidden_grad.astype(F32)
    gate_delta = hidden_grad * up_val * sigma * (1.0 + gate_val * (1.0 - sigma))
    up_delta = hidden_grad * silu
    both = jnp.concatenate([gate_delta.astype(BF), up_delta.astype(BF)], axis=1)
    sums_other = contract_rows(other, both).astype(BF)
    both, sums_other = tie(both, sums_other)
    sums_other = swap(sums_other)
    term = [contract_cols(both, m).astype(BF) for m in (both_w, both_w_other)]
    term = [t.reshape(8, 2, tokens, width).transpose(1, 0, 2, 3) for t in term]
    term = jnp.where(w == 0, jnp.stack(term, axis=1), jnp.stack(term[::-1], axis=1))
    term = lax.all_to_all(term, "core", 0, 0, tiled=True)
    term = term.astype(F32).sum(axis=0).astype(BF).reshape(16, tokens, width)
    term = lax.all_to_all(term, ("zw", "y"), 0, 0, tiled=True)
    gate_grad = (contract_rows(own, both[:, :units]) + sums_other[:, :units].astype(F32)).astype(BF)
    up_grad = (contract_rows(own, both[:, units:]) + sums_other[:, units:].astype(F32)).astype(BF)
    down_grad = (contract_rows(hidden, grads[:, :width]) + down_other.astype(F32)).astype(BF)
    term, gate_grad, up_grad = tie(term, gate_grad, up_grad)
    input_grad = term.astype(F32).reshape(2, 8, tokens, width).sum(axis=1).astype(BF)
    return (input_grad.reshape(2 * tokens, width), gate_grad, up_grad, down_grad)


def solution(mesh):
    fine = Mesh(mesh.devices.reshape(4, 4, 2, 8, 2), ("x", "zq", "zw", "y", "core"))
    row, col = ("x", "zq", "zw"), ("y", "core")
    return jax.shard_map(
        body,
        mesh=fine,
        in_specs=(
            P(col, row),
            P(col, row),
            P(row, col),
            P(row, col),
            P(row, col),
            P(row, col),
            P(col, row),
        ),
        out_specs=(P(col, row), P(row, col), P(row, col), P(col, row)),
        check_vma=False,
    )
```
